1024 devices in a mesh: dp: 32 (over y, x), fsdp: 32 (over z, core).
Axes of the slice: x: 4, y: 8, z: 16, core: 2. Of those that a mesh axis runs over, the one named last changes fastest.
Arguments:
- activations: bfloat16 [131072, 8192], P('dp', 'fsdp'), may hold values from -0.3984375 to 0.3984375
- out_grads: bfloat16 [131072, 1024], P('dp', 'fsdp'), may hold values from -0.3984375 to 0.3984375
- tile_domain: int32 [1024, 1], P('dp'), may hold values from 0 to 63
- adapter_a: bfloat16 [64, 16, 8192], P('dp', None, 'fsdp'), may hold values from -1.5 to 1.5
- adapter_b: bfloat16 [64, 16, 1024], P('dp', None, 'fsdp'), may hold values from -0.1875 to 0.1875
Outputs:
- grad_a: float32 [64, 16, 8192], P('dp', None, 'fsdp')
- grad_b: float32 [64, 16, 1024], P('dp', None, 'fsdp')
The draws below stay inside these ranges and needn't reach their ends.
All inputs are finite; a program needn't handle non-finite values.
Results may differ from the reference program's by a relative error of at most 0.0029.
Values may be sent and summed in bfloat16 or wider, within the bound.
No kernel may reach another device: no remote copies, remote signals or barrier semaphores. Data moves between devices by JAX's collectives and lax.ppermute only.
A program may use at most 32 MiB of HBM per device.

```python
import math
import jax
import jax.numpy as jnp
from jax import lax

D = 8192
KV = 1024
R = 16
TILE = 128
DOMAINS = 64
TOKENS = 131072
TILES = 1024


def steps_of(rng, extent, split, low, top_value):
    gain, own = 1.0, jax.random.fold_in(rng, 6)
    for dim, parts in split:
        heights = jnp.exp(jax.random.uniform(jax.random.fold_in(own, dim), (parts,), jnp.float32, low / len(split), top_value / len(split)))
        gain = gain * jnp.repeat(heights, extent[dim] // parts).reshape([-1 if axis == dim else 1 for axis in range(len(extent))])
    return gain


def picks_of(own_key, rows, amount, top, lift):
    sequence = jax.random.permutation(jax.random.fold_in(own_key, 1), amount)
    boost = sequence
    for power in range(3):
        boost = boost * boost // amount
    boost = boost * lift // amount
    lots = jax.random.randint(jax.random.fold_in(own_key, 2), (rows, amount), 0, 4096) + boost
    sure = jax.random.permutation(jax.random.fold_in(own_key, 3), rows)[jnp.arange(amount) % rows]
    lots = jnp.where(jnp.arange(rows)[:, None] == sure[None, :], 1 << 14, lots)
    score = lots * amount + jnp.arange(amount)
    return lax.top_k(score.astype(jnp.int32), top)[1].astype(jnp.int32)


def scatter_about(rng, shape, width, most, shards=(), held_as=jnp.bfloat16):
    entries = jax.random.normal(rng, shape, jnp.float32) * width
    if len(shards) > 0:
        entries = steps_of(rng, shape, shards, -0.22, 0.18) * entries
    return jnp.clip(entries, min=-most, max=most).astype(held_as)


def setup_inputs(seed: int = 0) -> dict:
    streams_of = jax.random.split(jax.random.key(seed), 6)
    activations = scatter_about(streams_of[0], (TOKENS, D), 0.05, 0.3984375, ((0, 32), (1, 32)))
    out_grads = scatter_about(streams_of[1], (TOKENS, KV), 0.05, 0.3984375, ((0, 32), (1, 32)))
    tile_domain = picks_of(streams_of[2], TILES, DOMAINS, 1, 256)
    adapter_a = scatter_about(streams_of[3], (DOMAINS, R, D), R ** -0.5, 1.5, ((0, 32), (2, 32)))
    adapter_b = scatter_about(streams_of[4], (DOMAINS, R, KV), KV ** -0.5, 0.1875, ((0, 32), (2, 32)))
    return {"activations": activations, "out_grads": out_grads, "tile_domain": tile_domain, "adapter_a": adapter_a, "adapter_b": adapter_b}


def reference(activations, out_grads, tile_domain, adapter_a, adapter_b):
    block = math.gcd(TILES, 8)
    count = TILES // block
    act = activations.reshape(count, block, TILE, D)
    grads = out_grads.reshape(count, block, TILE, KV)
    idents = tile_domain[:, 0].reshape(count, block)
    highest = lax.Precision.HIGHEST

    def step(carry, pieces):
        total_a, total_b = carry
        act_block, grad_block, id_block = pieces
        chosen_a = adapter_a[id_block].astype(jnp.float32)
        chosen_b = adapter_b[id_block].astype(jnp.float32)
        act_f = act_block.astype(jnp.float32)
        grad_f = grad_block.astype(jnp.float32)
        down = jnp.einsum('tkd,trd->tkr', act_f, chosen_a, precision=highest).astype(jnp.bfloat16)
        up = jnp.einsum('tkc,trc->tkr', grad_f, chosen_b, precision=highest).astype(jnp.bfloat16)
        a_terms = jnp.einsum('tkd,tkr->trd', act_f, up.astype(jnp.float32), precision=highest)
        b_terms = jnp.einsum('tkr,tkc->trc', down.astype(jnp.float32), grad_f, precision=highest)
        onehot = (id_block[:, None] == jnp.arange(DOMAINS, dtype=jnp.int32)[None, :]).astype(jnp.float32)
        total_a = total_a + jnp.einsum('te,trd->erd', onehot, a_terms, precision=highest)
        total_b = total_b + jnp.einsum('te,trc->erc', onehot, b_terms, precision=highest)
        return (total_a, total_b), None

    start = (jnp.zeros((DOMAINS, R, D), jnp.float32), jnp.zeros((DOMAINS, R, KV), jnp.float32))
    (total_a, total_b), unused = lax.scan(step, start, (act, grads, idents))
    return 2.0 * total_a, 2.0 * total_b
```

```python
import jax
import jax.numpy as jnp
from jax import lax
from jax.experimental import pallas as pl
from jax.experimental.pallas import tpu as pltpu
from jax.sharding import PartitionSpec as P

F32 = jnp.float32
BF16 = jnp.bfloat16
TILE = 128
RANK = 16
OWNERS = 32
DEPTH = 16
ROWS = 72

NT = (((1,), (1,)), ((), ()))
NN = (((1,), (0,)), ((), ()))
PARAMS = pltpu.CompilerParams(vmem_limit_bytes=32 * 1024 * 1024)
VMEM = pl.BlockSpec(memory_space=pltpu.VMEM)
SMEM = pl.BlockSpec(memory_space=pltpu.SMEM)


def call(kernel, out, specs, *operands, scratch=()):
    return pl.pallas_call(
        kernel,
        out_shape=out,
        in_specs=specs,
        out_specs=jax.tree.map(lambda _: VMEM, out),
        scratch_shapes=scratch,
        compiler_params=PARAMS,
    )(*operands)


def lane_block():
    return lax.broadcasted_iota(jnp.int32, (8, 128), 1) // 32


def pack_kernel(a_ref, b_ref, out_ref):
    pieces = []
    for i in range(2):
        pieces += [a_ref[i, :, 0:128], a_ref[i, :, 128:256]]
    rows = lax.broadcasted_iota(jnp.int32, (32, 128), 0)
    lanes = lax.broadcasted_iota(jnp.int32, (32, 128), 1)
    small = jnp.zeros((8, 128), F32)
    for i in range(2):
        for h in range(2):
            place = jnp.where(lanes == rows + 32 * (2 * i + h), 1.0, 0.0).astype(BF16)
            spread = lax.dot_general(b_ref[i], place, NN, preferred_element_type=F32)
            small = small + spread[8 * h : 8 * h + 8]
    big = jnp.concatenate(pieces, axis=0)
    small = small.astype(BF16)
    for o in range(OWNERS):
        out_ref[o, 0:64] = big
        out_ref[o, 64:72] = small


def tile_og(og_ref, tile):
    og = og_ref[:, pl.ds(pl.multiple_of(tile * TILE, TILE), TILE)]
    return jnp.concatenate([og, og, og, og], axis=0)


def tile_act(act_ref, tile):
    return act_ref[pl.ds(pl.multiple_of(tile * TILE, TILE), TILE), :]


def partial_kernel(ids_ref, w_ref, act_ref, og_ref, keep_ref, send_ref):
    core = lax.axis_index("fsdp") % 2
    block = lane_block()
    for out_ref, parity in ((send_ref, 1 - core), (keep_ref, core)):
        for z in range(DEPTH):
            tile = 2 * z + parity
            e = ids_ref[tile]
            o = e // 2
            i = e % 2
            a = w_ref[o, pl.ds(pl.multiple_of(i * 32, 32), 32), :]
            b = w_ref[o, 64:72, :].astype(F32)
            left = jnp.concatenate([a[0:16], a[16:32]], axis=1)
            down = lax.dot_general(left, tile_act(act_ref, tile), NT, preferred_element_type=F32)
            spread = jnp.concatenate(
                [jnp.where(block == 2 * i, b, 0.0), jnp.where(block == 2 * i + 1, b, 0.0)], axis=0
            ).astype(BF16)
            up = lax.dot_general(spread, tile_og(og_ref, tile), NN, preferred_element_type=F32)
            out_ref[z, 0:16] = down
            out_ref[z, 16:32] = up


def round_kernel(in_ref, out_ref):
    total = in_ref[0]
    for z in range(1, DEPTH):
        total = total + in_ref[z]
    total = total.astype(BF16)
    for z in range(DEPTH):
        out_ref[z] = total


def grad_kernel(ids_ref, act_ref, og_ref, own_ref, other_ref, out_ref, acc_ref, ga_ref, gb_ref):
    core = lax.axis_index("fsdp") % 2
    acc_ref[...] = jnp.zeros_like(acc_ref)
    block = lane_block()
    for p, (in_ref, parity) in enumerate(((own_ref, core), (other_ref, 1 - core))):
        for z in range(DEPTH):
            tile = 2 * z + parity
            down = in_ref[z, 0:16]
            up = in_ref[z, 16:32]
            ga_ref[p * DEPTH + z] = lax.dot_general(up, tile_act(act_ref, tile), NN, preferred_element_type=F32)
            gb_ref[p * DEPTH + z] = lax.dot_general(down, tile_og(og_ref, tile), NT, preferred_element_type=F32)
    for p, parity in enumerate((core, 1 - core)):
        for z in range(DEPTH):
            e = ids_ref[2 * z + parity]
            o = e // 2
            i = e % 2
            ga = ga_ref[p * DEPTH + z]
            gb = gb_ref[p * DEPTH + z]
            at = pl.ds(pl.multiple_of(i * 32, 32), 32)
            acc_ref[o, at, :] += jnp.concatenate([ga[:, 0:128], ga[:, 128:256]], axis=0)
            acc_ref[o, 64:72, :] += jnp.where(block == 2 * i, gb[0:8], 0.0) + jnp.where(block == 2 * i + 1, gb[8:16], 0.0)
    for o in range(OWNERS):
        out_ref[o] = (2.0 * acc_ref[o]).astype(BF16)


def final_kernel(in_ref, ga_ref, gb_ref):
    total = in_ref[0].astype(F32)
    for o in range(1, OWNERS):
        total = total + in_ref[o].astype(F32)
    for i in range(2):
        for h in range(2):
            ga_ref[i, :, 128 * h : 128 * h + 128] = total[32 * i + 16 * h : 32 * i + 16 * h + 16]
            k = 2 * i + h
            gb_ref[i, 8 * h : 8 * h + 8, :] = total[64:72, 32 * k : 32 * k + 32]


def shards(activations, out_grads, tile_domain, adapter_a, adapter_b):
    shape = jax.ShapeDtypeStruct
    ids = tile_domain[:, 0]
    og = out_grads.T
    pair = [(f, f ^ 1) for f in range(2 * DEPTH)]
    columns = [[2 * z + c for z in range(DEPTH)] for c in range(2)]
    along_z = lambda x: lax.all_to_all(x, "fsdp", 0, 0, tiled=True, axis_index_groups=columns)

    packed = call(pack_kernel, shape((OWNERS, ROWS, 128), BF16), [VMEM, VMEM], adapter_a, adapter_b)
    weights = lax.all_to_all(packed, "dp", 0, 0, tiled=True)
    part = shape((DEPTH, 32, 128), F32)
    keep, send = call(partial_kernel, (part, part), [SMEM, VMEM, VMEM, VMEM], ids, weights, activations, og)
    chip = keep + lax.ppermute(send, "fsdp", pair)
    full = call(round_kernel, shape((DEPTH, 32, 128), BF16), [VMEM], along_z(chip))
    own = along_z(full)
    other = lax.ppermute(own, "fsdp", pair)
    grads = call(
        grad_kernel,
        shape((OWNERS, ROWS, 128), BF16),
        [SMEM, VMEM, VMEM, VMEM, VMEM],
        ids,
        activations,
        og,
        own,
        other,
        scratch=[
            pltpu.VMEM((OWNERS, ROWS, 128), F32),
            pltpu.VMEM((2 * DEPTH, 16, 256), F32),
            pltpu.VMEM((2 * DEPTH, 16, 128), F32),
        ],
    )
    summed = lax.all_to_all(grads, "dp", 0, 0, tiled=True)
    return call(final_kernel, (shape((2, RANK, 256), F32), shape((2, RANK, 32), F32)), [VMEM], summed)


def solution(mesh):
    placed = (
        P("dp", "fsdp"),
        P("dp", "fsdp"),
        P("dp", None),
        P("dp", None, "fsdp"),
        P("dp", None, "fsdp"),
    )
    return jax.shard_map(
        shards,
        mesh=mesh,
        in_specs=placed,
        out_specs=(P("dp", None, "fsdp"), P("dp", None, "fsdp")),
        check_vma=False,
    )
```

```python
import jax
import jax.numpy as jnp
from jax import lax
from jax.experimental import pallas as pl
from jax.experimental.pallas import tpu as pltpu
from jax.sharding import PartitionSpec as P

F32 = jnp.float32
BF16 = jnp.bfloat16
F16 = jnp.float16
TILE = 128
RANK = 16
OWNERS = 32
NEAR = 8
FAR = 4
TILES = NEAR * FAR
ROWS = 72
SENT = FAR * 32 + 8
TOP = 16384.0

NT = (((1,), (1,)), ((), ()))
NN = (((1,), (0,)), ((), ()))
VMEM = pl.BlockSpec(memory_space=pltpu.VMEM)
SMEM = pl.BlockSpec(memory_space=pltpu.SMEM)
MIB = 1024 * 1024
AHEAD = pl.CostEstimate(flops=10_000_000_000, bytes_accessed=20_000_000, transcendentals=0)


def call(kernel, out, specs, *operands, scratch=(), cost=None):
    return pl.pallas_call(
        kernel,
        out_shape=out,
        in_specs=specs,
        out_specs=jax.tree.map(lambda _: VMEM, out),
        scratch_shapes=scratch,
        cost_estimate=cost,
        compiler_params=pltpu.CompilerParams(vmem_limit_bytes=32 * MIB),
    )(*operands)


def lane_block():
    return lax.broadcasted_iota(jnp.int32, (8, 128), 1) // 32


def pack_kernel(a_ref, b_ref, out_ref):
    pieces = []
    for i in range(2):
        pieces += [a_ref[i, :, 0:128], a_ref[i, :, 128:256]]
    rows = lax.broadcasted_iota(jnp.int32, (32, 128), 0)
    lanes = lax.broadcasted_iota(jnp.int32, (32, 128), 1)
    small = jnp.zeros((8, 128), F32)
    for i in range(2):
        for h in range(2):
            place = jnp.where(lanes == rows + 32 * (2 * i + h), 1.0, 0.0).astype(BF16)
            spread = lax.dot_general(b_ref[i], place, NN, preferred_element_type=F32)
            small = small + spread[8 * h : 8 * h + 8]
    big = jnp.concatenate(pieces, axis=0)
    small = small.astype(BF16)
    for o in range(OWNERS):
        out_ref[o, 0:64] = big
        out_ref[o, 64:72] = small


def tile_og(og_ref, tile):
    og = og_ref[:, tile * TILE : tile * TILE + TILE]
    return jnp.concatenate([og, og, og, og], axis=0)


def tile_act(act_ref, tile):
    return act_ref[tile * TILE : tile * TILE + TILE, :]


def scale_of(down_top, up_top):
    down = jnp.broadcast_to(jnp.max(down_top, axis=(0, 1), keepdims=True), (8, 128))
    up = jnp.broadcast_to(jnp.max(up_top, axis=(0, 1), keepdims=True), (8, 128))
    both = jnp.where(lax.broadcasted_iota(jnp.int32, (8, 128), 0) == 0, down, up)
    root = jnp.sqrt(jnp.sqrt(both))
    return jnp.maximum(root, 2.0**-13).astype(BF16).astype(F32)


def fourth(root):
    square = root * root
    return square * square


def widen(row):
    return jnp.broadcast_to(row, (16, 128))


def partial_kernel(ids_ref, w_ref, act_ref, og_ref, out_ref, part_ref):
    block = lane_block()
    down_top = jnp.zeros((RANK, TILE), F32)
    up_top = jnp.zeros((RANK, TILE), F32)
    for tile in range(TILES):
        e = ids_ref[tile]
        o = e // 2
        i = e % 2
        a = w_ref[o, pl.ds(pl.multiple_of(i * 32, 32), 32), :]
        b = w_ref[o, 64:72, :].astype(F32)
        left = jnp.concatenate([a[0:16], a[16:32]], axis=1)
        down = lax.dot_general(left, tile_act(act_ref, tile), NT, preferred_element_type=F32)
        spread = jnp.concatenate(
            [jnp.where(block == 2 * i, b, 0.0), jnp.where(block == 2 * i + 1, b, 0.0)], axis=0
        ).astype(BF16)
        up = lax.dot_general(spread, tile_og(og_ref, tile), NN, preferred_element_type=F32)
        part_ref[tile, 0:16] = down
        part_ref[tile, 16:32] = up
        down_top = jnp.maximum(down_top, jnp.abs(down))
        up_top = jnp.maximum(up_top, jnp.abs(up))
    root = scale_of(down_top, up_top)
    factor = TOP / fourth(root)
    down_factor, up_factor = widen(factor[0:1]), widen(factor[1:2])
    for q in range(NEAR):
        for a in range(FAR):
            tile = NEAR * a + q
            out_ref[q, 32 * a : 32 * a + 16] = part_ref[tile, 0:16] * down_factor
            out_ref[q, 32 * a + 16 : 32 * a + 32] = part_ref[tile, 16:32] * up_factor
        out_ref[q, FAR * 32 : SENT] = root


def summed_parts(in_ref, count):
    downs = [jnp.zeros((RANK, TILE), F32)] * FAR
    ups = [jnp.zeros((RANK, TILE), F32)] * FAR
    for q in range(count):
        factor = fourth(in_ref[q, FAR * 32 : SENT]) * (1.0 / TOP)
        down_factor, up_factor = widen(factor[0:1]), widen(factor[1:2])
        for a in range(FAR):
            downs[a] = downs[a] + in_ref[q, 32 * a : 32 * a + 16] * down_factor
            ups[a] = ups[a] + in_ref[q, 32 * a + 16 : 32 * a + 32] * up_factor
    return downs, ups


def near_kernel(in_ref, out_ref):
    downs, ups = summed_parts(in_ref, NEAR)
    down_top, up_top = jnp.abs(downs[0]), jnp.abs(ups[0])
    for a in range(1, FAR):
        down_top = jnp.maximum(down_top, jnp.abs(downs[a]))
        up_top = jnp.maximum(up_top, jnp.abs(ups[a]))
    root = scale_of(down_top, up_top)
    factor = TOP / fourth(root)
    down_factor, up_factor = widen(factor[0:1]), widen(factor[1:2])
    for a in range(FAR):
        down = downs[a] * down_factor
        up = ups[a] * up_factor
        for f in range(FAR):
            out_ref[f, 32 * a : 32 * a + 16] = down
            out_ref[f, 32 * a + 16 : 32 * a + 32] = up
    for f in range(FAR):
        out_ref[f, FAR * 32 : SENT] = root


def round_kernel(in_ref, out_ref):
    downs, ups = summed_parts(in_ref, FAR)
    for a in range(FAR):
        down = downs[a].astype(BF16)
        up = ups[a].astype(BF16)
        for q in range(NEAR):
            out_ref[q, 32 * a : 32 * a + 16] = down
            out_ref[q, 32 * a + 16 : 32 * a + 32] = up


def grad_kernel(ids_ref, act_ref, og_ref, in_ref, out_ref, acc_ref, ga_ref, gb_ref):
    acc_ref[...] = jnp.zeros_like(acc_ref)
    block = lane_block()
    for tile in range(TILES):
        q, a = tile % NEAR, tile // NEAR
        down = in_ref[q, 32 * a : 32 * a + 16]
        up = in_ref[q, 32 * a + 16 : 32 * a + 32]
        ga_ref[tile] = lax.dot_general(up, tile_act(act_ref, tile), NN, preferred_element_type=F32)
        gb_ref[tile] = lax.dot_general(down, tile_og(og_ref, tile), NT, preferred_element_type=F32)
    for tile in range(TILES):
        e = ids_ref[tile]
        o = e // 2
        i = e % 2
        ga = ga_ref[tile]
        gb = gb_ref[tile]
        at = pl.ds(pl.multiple_of(i * 32, 32), 32)
        acc_ref[o, at, :] += jnp.concatenate([ga[:, 0:128], ga[:, 128:256]], axis=0)
        acc_ref[o, 64:72, :] += jnp.where(block == 2 * i, gb[0:8], 0.0) + jnp.where(block == 2 * i + 1, gb[8:16], 0.0)
    for o in range(OWNERS):
        out_ref[o] = (2.0 * acc_ref[o]).astype(BF16)


def final_kernel(in_ref, ga_ref, gb_ref):
    total = in_ref[0].astype(F32)
    for o in range(1, OWNERS):
        total = total + in_ref[o].astype(F32)
    for i in range(2):
        for h in range(2):
            ga_ref[i, :, 128 * h : 128 * h + 128] = total[32 * i + 16 * h : 32 * i + 16 * h + 16]
            k = 2 * i + h
            gb_ref[i, 8 * h : 8 * h + 8, :] = total[64:72, 32 * k : 32 * k + 32]


def shards(activations, out_grads, tile_domain, adapter_a, adapter_b):
    shape = jax.ShapeDtypeStruct
    ids = tile_domain[:, 0]
    og = out_grads.T
    near_groups = [[NEAR * f + q for q in range(NEAR)] for f in range(FAR)]
    far_groups = [[NEAR * f + q for f in range(FAR)] for q in range(NEAR)]
    near = lambda x: lax.all_to_all(x, "fsdp", 0, 0, tiled=True, axis_index_groups=near_groups)
    far = lambda x: lax.all_to_all(x, "fsdp", 0, 0, tiled=True, axis_index_groups=far_groups)

    packed = call(
        pack_kernel,
        shape((OWNERS, ROWS, 128), BF16),
        [VMEM, VMEM],
        adapter_a,
        adapter_b,
        cost=AHEAD,
    )
    weights = lax.all_to_all(packed, "dp", 0, 0, tiled=True)
    part = call(
        partial_kernel,
        shape((NEAR, SENT, 128), F32),
        [SMEM, VMEM, VMEM, VMEM],
        ids,
        weights,
        activations,
        og,
        scratch=[pltpu.VMEM((TILES, 32, 128), F32)],
    )
    part = near(part.astype(F16)).astype(F32)
    part = call(near_kernel, shape((FAR, SENT, 128), F32), [VMEM], part)
    part = far(part.astype(F16)).astype(F32)
    full = near(call(round_kernel, shape((NEAR, FAR * 32, 128), BF16), [VMEM], part))
    grads = call(
        grad_kernel,
        shape((OWNERS, ROWS, 128), BF16),
        [SMEM, VMEM, VMEM, VMEM],
        ids,
        activations,
        og,
        full,
        scratch=[
            pltpu.VMEM((OWNERS, ROWS, 128), F32),
            pltpu.VMEM((TILES, 16, 256), F32),
            pltpu.VMEM((TILES, 16, 128), F32),
        ],
    )
    summed = lax.all_to_all(grads, "dp", 0, 0, tiled=True)
    return call(final_kernel, (shape((2, RANK, 256), F32), shape((2, RANK, 32), F32)), [VMEM], summed)


def solution(mesh):
    placed = (
        P("dp", "fsdp"),
        P("dp", "fsdp"),
        P("dp", None),
        P("dp", None, "fsdp"),
        P("dp", None, "fsdp"),
    )
    return jax.shard_map(
        shards,
        mesh=mesh,
        in_specs=placed,
        out_specs=(P("dp", None, "fsdp"), P("dp", None, "fsdp")),
        check_vma=False,
    )
```

```python
import functools

import jax
import jax.numpy as jnp
from jax import lax
from jax.experimental import pallas as pl
from jax.experimental.pallas import tpu as pltpu
from jax.sharding import PartitionSpec as P

F32 = jnp.float32
BF16 = jnp.bfloat16
F16 = jnp.float16
TILE = 128
RANK = 16
OWNERS = 32
NEAR = 4
FAR = 4
SHARE = NEAR * FAR
ROWS = 72
SENT = FAR * 32 + 8
TOP = 16384.0

NT = (((1,), (1,)), ((), ()))
NN = (((1,), (0,)), ((), ()))
VMEM = pl.BlockSpec(memory_space=pltpu.VMEM)
SMEM = pl.BlockSpec(memory_space=pltpu.SMEM)
MIB = 1024 * 1024
AHEAD = pl.CostEstimate(flops=10_000_000_000, bytes_accessed=20_000_000, transcendentals=0)
HALF = pl.CostEstimate(flops=2_000_000_000, bytes_accessed=4_000_000, transcendentals=0)


def call(kernel, out, specs, *operands, scratch=(), cost=None):
    return pl.pallas_call(
        kernel,
        out_shape=out,
        in_specs=specs,
        out_specs=jax.tree.map(lambda _: VMEM, out),
        scratch_shapes=scratch,
        cost_estimate=cost,
        compiler_params=pltpu.CompilerParams(vmem_limit_bytes=32 * MIB),
    )(*operands)


def lane_block():
    return lax.broadcasted_iota(jnp.int32, (8, 128), 1) // 32


def pack_kernel(a_ref, b_ref, out_ref):
    pieces = []
    for i in range(2):
        pieces += [a_ref[i, :, 0:128], a_ref[i, :, 128:256]]
    rows = lax.broadcasted_iota(jnp.int32, (32, 128), 0)
    lanes = lax.broadcasted_iota(jnp.int32, (32, 128), 1)
    small = jnp.zeros((8, 128), F32)
    for i in range(2):
        for h in range(2):
            place = jnp.where(lanes == rows + 32 * (2 * i + h), 1.0, 0.0).astype(BF16)
            spread = lax.dot_general(b_ref[i], place, NN, preferred_element_type=F32)
            small = small + spread[8 * h : 8 * h + 8]
    big = jnp.concatenate(pieces, axis=0)
    small = small.astype(BF16)
    for o in range(OWNERS):
        out_ref[o, 0:64] = big
        out_ref[o, 64:72] = small


def tile_at(b, a, parity):
    return 2 * NEAR * a + 2 * b + parity


def tile_og(og_ref, tile):
    og = og_ref[:, pl.ds(pl.multiple_of(tile * TILE, TILE), TILE)]
    return jnp.concatenate([og, og, og, og], axis=0)


def tile_act(act_ref, tile):
    return act_ref[pl.ds(pl.multiple_of(tile * TILE, TILE), TILE), :]


def scale_of(down_top, up_top):
    down = jnp.broadcast_to(jnp.max(down_top, axis=(0, 1), keepdims=True), (8, 128))
    up = jnp.broadcast_to(jnp.max(up_top, axis=(0, 1), keepdims=True), (8, 128))
    both = jnp.where(lax.broadcasted_iota(jnp.int32, (8, 128), 0) == 0, down, up)
    root = jnp.sqrt(jnp.sqrt(both))
    return jnp.maximum(root, 2.0**-13).astype(BF16).astype(F32)


def fourth(root):
    square = root * root
    return square * square


def widen(row):
    return jnp.broadcast_to(row, (16, 128))


def parity_of(own):
    core = lax.axis_index("fsdp") % 2
    return core if own else 1 - core


def partial_kernel(own, ids_ref, w_ref, act_ref, og_ref, out_ref):
    parity = parity_of(own)
    block = lane_block()
    for b in range(NEAR):
        for a in range(FAR):
            tile = tile_at(b, a, parity)
            e = ids_ref[tile]
            o = e // 2
            i = e % 2
            w = w_ref[o, pl.ds(pl.multiple_of(i * 32, 32), 32), :]
            small = w_ref[o, 64:72, :].astype(F32)
            left = jnp.concatenate([w[0:16], w[16:32]], axis=1)
            down = lax.dot_general(left, tile_act(act_ref, tile), NT, preferred_element_type=F32)
            spread = jnp.concatenate(
                [jnp.where(block == 2 * i, small, 0.0), jnp.where(block == 2 * i + 1, small, 0.0)], axis=0
            ).astype(BF16)
            up = lax.dot_general(spread, tile_og(og_ref, tile), NN, preferred_element_type=F32)
            out_ref[b, 32 * a : 32 * a + 16] = down
            out_ref[b, 32 * a + 16 : 32 * a + 32] = up


def chip_kernel(keep_ref, other_ref, out_ref, part_ref):
    down_top = jnp.zeros((RANK, TILE), F32)
    up_top = jnp.zeros((RANK, TILE), F32)
    for b in range(NEAR):
        part = keep_ref[b] + other_ref[b]
        part_ref[b] = part
        for a in range(FAR):
            down_top = jnp.maximum(down_top, jnp.abs(part[32 * a : 32 * a + 16]))
            up_top = jnp.maximum(up_top, jnp.abs(part[32 * a + 16 : 32 * a + 32]))
    root = scale_of(down_top, up_top)
    factor = TOP / fourth(root)
    both = jnp.concatenate([widen(factor[0:1]), widen(factor[1:2])] * FAR, axis=0)
    for b in range(NEAR):
        out_ref[b, 0 : FAR * 32] = part_ref[b] * both
        out_ref[b, FAR * 32 : SENT] = root


def summed_parts(in_ref, count):
    downs = [jnp.zeros((RANK, TILE), F32)] * FAR
    ups = [jnp.zeros((RANK, TILE), F32)] * FAR
    for q in range(count):
        factor = fourth(in_ref[q, FAR * 32 : SENT]) * (1.0 / TOP)
        down_factor, up_factor = widen(factor[0:1]), widen(factor[1:2])
        for a in range(FAR):
            downs[a] = downs[a] + in_ref[q, 32 * a : 32 * a + 16] * down_factor
            ups[a] = ups[a] + in_ref[q, 32 * a + 16 : 32 * a + 32] * up_factor
    return downs, ups


def near_kernel(in_ref, out_ref):
    downs, ups = summed_parts(in_ref, NEAR)
    down_top, up_top = jnp.abs(downs[0]), jnp.abs(ups[0])
    for a in range(1, FAR):
        down_top = jnp.maximum(down_top, jnp.abs(downs[a]))
        up_top = jnp.maximum(up_top, jnp.abs(ups[a]))
    root = scale_of(down_top, up_top)
    factor = TOP / fourth(root)
    down_factor, up_factor = widen(factor[0:1]), widen(factor[1:2])
    for a in range(FAR):
        down = downs[a] * down_factor
        up = ups[a] * up_factor
        for f in range(FAR):
            out_ref[f, 32 * a : 32 * a + 16] = down
            out_ref[f, 32 * a + 16 : 32 * a + 32] = up
    for f in range(FAR):
        out_ref[f, FAR * 32 : SENT] = root


def round_kernel(in_ref, out_ref):
    downs, ups = summed_parts(in_ref, FAR)
    for a in range(FAR):
        down = downs[a].astype(BF16)
        up = ups[a].astype(BF16)
        for q in range(NEAR):
            out_ref[q, 32 * a : 32 * a + 16] = down
            out_ref[q, 32 * a + 16 : 32 * a + 32] = up


def add_grads(own, ids_ref, act_ref, og_ref, in_ref, acc_ref, ga_ref, gb_ref):
    parity = parity_of(own)
    block = lane_block()
    places = [(b, a) for b in range(NEAR) for a in range(FAR)]
    for n, (b, a) in enumerate(places):
        tile = tile_at(b, a, parity)
        down = in_ref[b, 32 * a : 32 * a + 16]
        up = in_ref[b, 32 * a + 16 : 32 * a + 32]
        ga_ref[n] = lax.dot_general(up, tile_act(act_ref, tile), NN, preferred_element_type=F32)
        gb_ref[n] = lax.dot_general(down, tile_og(og_ref, tile), NT, preferred_element_type=F32)
    for n, (b, a) in enumerate(places):
        e = ids_ref[tile_at(b, a, parity)]
        o = e // 2
        i = e % 2
        ga = ga_ref[n]
        gb = gb_ref[n]
        at = pl.ds(pl.multiple_of(i * 32, 32), 32)
        acc_ref[o, at, :] += jnp.concatenate([ga[:, 0:128], ga[:, 128:256]], axis=0)
        acc_ref[o, 64:72, :] += jnp.where(block == 2 * i, gb[0:8], 0.0) + jnp.where(block == 2 * i + 1, gb[8:16], 0.0)


def first_kernel(ids_ref, act_ref, og_ref, in_ref, acc_ref, ga_ref, gb_ref):
    acc_ref[...] = jnp.zeros_like(acc_ref)
    add_grads(True, ids_ref, act_ref, og_ref, in_ref, acc_ref, ga_ref, gb_ref)


def second_kernel(ids_ref, act_ref, og_ref, in_ref, sum_ref, out_ref, acc_ref, ga_ref, gb_ref):
    acc_ref[...] = sum_ref[...]
    add_grads(False, ids_ref, act_ref, og_ref, in_ref, acc_ref, ga_ref, gb_ref)
    for o in range(OWNERS):
        out_ref[o] = (2.0 * acc_ref[o]).astype(BF16)


def final_kernel(in_ref, ga_ref, gb_ref):
    total = in_ref[0].astype(F32)
    for o in range(1, OWNERS):
        total = total + in_ref[o].astype(F32)
    for i in range(2):
        for h in range(2):
            ga_ref[i, :, 128 * h : 128 * h + 128] = total[32 * i + 16 * h : 32 * i + 16 * h + 16]
            k = 2 * i + h
            gb_ref[i, 8 * h : 8 * h + 8, :] = total[64:72, 32 * k : 32 * k + 32]


def shards(activations, out_grads, tile_domain, adapter_a, adapter_b):
    shape = jax.ShapeDtypeStruct
    ids = tile_domain[:, 0]
    og = out_grads.T
    pair = [(f, f ^ 1) for f in range(2 * SHARE)]
    near_groups = [[2 * (NEAR * a + b) + c for b in range(NEAR)] for a in range(FAR) for c in range(2)]
    far_groups = [[2 * (NEAR * a + b) + c for a in range(FAR)] for b in range(NEAR) for c in range(2)]
    near = lambda x: lax.all_to_all(x, "fsdp", 0, 0, tiled=True, axis_index_groups=near_groups)
    far = lambda x: lax.all_to_all(x, "fsdp", 0, 0, tiled=True, axis_index_groups=far_groups)
    swap = lambda x: lax.ppermute(x, "fsdp", pair)

    packed = call(
        pack_kernel,
        shape((OWNERS, ROWS, 128), BF16),
        [VMEM, VMEM],
        adapter_a,
        adapter_b,
        cost=AHEAD,
    )
    weights = lax.all_to_all(packed, "dp", 0, 0, tiled=True)
    inputs = (ids, weights, activations, og)
    part = shape((NEAR, FAR * 32, 128), F32)
    kinds = [SMEM, VMEM, VMEM, VMEM]
    send = call(functools.partial(partial_kernel, False), part, kinds, *inputs, cost=HALF)
    keep = call(functools.partial(partial_kernel, True), part, kinds, *inputs, cost=HALF)
    scaled = shape((NEAR, SENT, 128), F32)
    chip = call(chip_kernel, scaled, [VMEM, VMEM], keep, swap(send), scratch=[pltpu.VMEM(part.shape, F32)])
    chip = near(chip.astype(F16)).astype(F32)
    part = call(near_kernel, shape((FAR, SENT, 128), F32), [VMEM], chip)
    part = far(part.astype(F16)).astype(F32)
    full = near(call(round_kernel, shape((NEAR, FAR * 32, 128), BF16), [VMEM], part))
    terms = [pltpu.VMEM((SHARE, 16, 256), F32), pltpu.VMEM((SHARE, 16, 128), F32)]
    total = (OWNERS, ROWS, 128)
    inputs = (ids, activations, og)
    grads = call(first_kernel, shape(total, F32), kinds, *inputs, full, scratch=terms, cost=HALF)
    grads = call(
        second_kernel, shape(total, BF16), kinds + [VMEM], *inputs, swap(full), grads, scratch=[pltpu.VMEM(total, F32)] + terms
    )
    summed = lax.all_to_all(grads, "dp", 0, 0, tiled=True)
    return call(final_kernel, (shape((2, RANK, 256), F32), shape((2, RANK, 32), F32)), [VMEM], summed)


def solution(mesh):
    placed = (
        P("dp", "fsdp"),
        P("dp", "fsdp"),
        P("dp", None),
        P("dp", None, "fsdp"),
        P("dp", None, "fsdp"),
    )
    return jax.shard_map(
        shards,
        mesh=mesh,
        in_specs=placed,
        out_specs=(P("dp", None, "fsdp"), P("dp", None, "fsdp")),
        check_vma=False,
    )
```

```python
import functools

import jax
import jax.numpy as jnp
from jax import lax
from jax.experimental import pallas as pl
from jax.experimental.pallas import tpu as pltpu
from jax.sharding import PartitionSpec as P

F32 = jnp.float32
BF16 = jnp.bfloat16
F16 = jnp.float16
TILE = 128
RANK = 16
OWNERS = 32
NEAR = 4
FAR = 4
SHARE = NEAR * FAR
ROWS = 72
SENT = FAR * 32 + 8
TOP = 16384.0

NT = (((1,), (1,)), ((), ()))
NN = (((1,), (0,)), ((), ()))
VMEM = pl.BlockSpec(memory_space=pltpu.VMEM)
MIB = 1024 * 1024
AHEAD = pl.CostEstimate(flops=10_000_000_000, bytes_accessed=20_000_000, transcendentals=0)
HALF = pl.CostEstimate(flops=2_000_000_000, bytes_accessed=4_000_000, transcendentals=0)


def call(kernel, out, specs, *operands, scratch=(), cost=None):
    return pl.pallas_call(
        kernel,
        out_shape=out,
        in_specs=specs,
        out_specs=jax.tree.map(lambda _: VMEM, out),
        scratch_shapes=scratch,
        cost_estimate=cost,
        compiler_params=pltpu.CompilerParams(vmem_limit_bytes=32 * MIB),
    )(*operands)


def lane_block():
    return lax.broadcasted_iota(jnp.int32, (8, 128), 1) // 32


def pack_kernel(ab_ref, out_ref):
    pieces = []
    for i in range(2):
        pieces += [ab_ref[i, :, 0:128], ab_ref[i, :, 128:256]]
    rows = lax.broadcasted_iota(jnp.int32, (32, 128), 0)
    lanes = lax.broadcasted_iota(jnp.int32, (32, 128), 1)
    small = jnp.zeros((8, 128), F32)
    for i in range(2):
        for h in range(2):
            place = jnp.where(lanes == rows + 32 * (2 * i + h), 1.0, 0.0).astype(BF16)
            spread = lax.dot_general(ab_ref[i, :, 256:288], place, NN, preferred_element_type=F32)
            small = small + spread[8 * h : 8 * h + 8]
    big = jnp.concatenate(pieces, axis=0)
    small = small.astype(BF16)
    for o in range(OWNERS):
        out_ref[o, 0:64] = big
        out_ref[o, 64:72] = small


def tile_at(b, a, parity):
    return 2 * NEAR * a + 2 * b + parity


def domains_of(ids_ref, parity):
    ids = ids_ref[...]
    return [jnp.where(parity == 1, ids[0, 2 * n + 1], ids[0, 2 * n]) for n in range(SHARE)]


def tile_og(og_ref, tile):
    og = og_ref[:, pl.ds(pl.multiple_of(tile * TILE, TILE), TILE)]
    return jnp.concatenate([og, og, og, og], axis=0)


def tile_act(act_ref, tile):
    return act_ref[pl.ds(pl.multiple_of(tile * TILE, TILE), TILE), :]


def scale_of(down_top, up_top):
    down = jnp.broadcast_to(jnp.max(down_top, axis=(0, 1), keepdims=True), (8, 128))
    up = jnp.broadcast_to(jnp.max(up_top, axis=(0, 1), keepdims=True), (8, 128))
    both = jnp.where(lax.broadcasted_iota(jnp.int32, (8, 128), 0) == 0, down, up)
    root = jnp.sqrt(jnp.sqrt(both))
    return jnp.maximum(root, 2.0**-13).astype(BF16).astype(F32)


def fourth(root):
    square = root * root
    return square * square


def widen(row):
    return jnp.broadcast_to(row, (16, 128))


def parity_of(own):
    core = lax.axis_index("fsdp") % 2
    return core if own else 1 - core


def partial_kernel(own, ids_ref, w_ref, act_ref, og_ref, out_ref):
    parity = parity_of(own)
    domains = domains_of(ids_ref, parity)
    block = lane_block()
    for b in range(NEAR):
        for a in range(FAR):
            tile = tile_at(b, a, parity)
            e = domains[NEAR * a + b]
            o = e // 2
            i = e % 2
            w = w_ref[o, pl.ds(pl.multiple_of(i * 32, 32), 32), :]
            small = w_ref[o, 64:72, :].astype(F32)
            left = jnp.concatenate([w[0:16], w[16:32]], axis=1)
            down = lax.dot_general(left, tile_act(act_ref, tile), NT, preferred_element_type=F32)
            spread = jnp.concatenate(
                [jnp.where(block == 2 * i, small, 0.0), jnp.where(block == 2 * i + 1, small, 0.0)], axis=0
            ).astype(BF16)
            up = lax.dot_general(spread, tile_og(og_ref, tile), NN, preferred_element_type=F32)
            out_ref[b, 32 * a : 32 * a + 16] = down
            out_ref[b, 32 * a + 16 : 32 * a + 32] = up


def chip_kernel(keep_ref, other_ref, out_ref, part_ref):
    down_top = jnp.zeros((RANK, TILE), F32)
    up_top = jnp.zeros((RANK, TILE), F32)
    for b in range(NEAR):
        part = keep_ref[b] + other_ref[b]
        part_ref[b] = part
        for a in range(FAR):
            down_top = jnp.maximum(down_top, jnp.abs(part[32 * a : 32 * a + 16]))
            up_top = jnp.maximum(up_top, jnp.abs(part[32 * a + 16 : 32 * a + 32]))
    root = scale_of(down_top, up_top)
    factor = TOP / fourth(root)
    both = jnp.concatenate([widen(factor[0:1]), widen(factor[1:2])] * FAR, axis=0)
    for b in range(NEAR):
        out_ref[b, 0 : FAR * 32] = part_ref[b] * both
        out_ref[b, FAR * 32 : SENT] = root


def summed_parts(in_ref, count):
    downs = [jnp.zeros((RANK, TILE), F32)] * FAR
    ups = [jnp.zeros((RANK, TILE), F32)] * FAR
    for q in range(count):
        factor = fourth(in_ref[q, FAR * 32 : SENT]) * (1.0 / TOP)
        down_factor, up_factor = widen(factor[0:1]), widen(factor[1:2])
        for a in range(FAR):
            downs[a] = downs[a] + in_ref[q, 32 * a : 32 * a + 16] * down_factor
            ups[a] = ups[a] + in_ref[q, 32 * a + 16 : 32 * a + 32] * up_factor
    return downs, ups


def near_kernel(in_ref, out_ref):
    downs, ups = summed_parts(in_ref, NEAR)
    down_top, up_top = jnp.abs(downs[0]), jnp.abs(ups[0])
    for a in range(1, FAR):
        down_top = jnp.maximum(down_top, jnp.abs(downs[a]))
        up_top = jnp.maximum(up_top, jnp.abs(ups[a]))
    root = scale_of(down_top, up_top)
    factor = TOP / fourth(root)
    down_factor, up_factor = widen(factor[0:1]), widen(factor[1:2])
    for a in range(FAR):
        down = downs[a] * down_factor
        up = ups[a] * up_factor
        for f in range(FAR):
            out_ref[f, 32 * a : 32 * a + 16] = down
            out_ref[f, 32 * a + 16 : 32 * a + 32] = up
    for f in range(FAR):
        out_ref[f, FAR * 32 : SENT] = root


def round_kernel(in_ref, out_ref):
    downs, ups = summed_parts(in_ref, FAR)
    for a in range(FAR):
        down = downs[a].astype(BF16)
        up = ups[a].astype(BF16)
        for q in range(NEAR):
            out_ref[q, 32 * a : 32 * a + 16] = down
            out_ref[q, 32 * a + 16 : 32 * a + 32] = up


def add_grads(own, ids_ref, act_ref, og_ref, in_ref, acc_ref, ga_ref, gb_ref):
    parity = parity_of(own)
    domains = domains_of(ids_ref, parity)
    block = lane_block()
    places = [(b, a) for b in range(NEAR) for a in range(FAR)]
    for n, (b, a) in enumerate(places):
        tile = tile_at(b, a, parity)
        down = in_ref[b, 32 * a : 32 * a + 16]
        up = in_ref[b, 32 * a + 16 : 32 * a + 32]
        ga_ref[n] = lax.dot_general(up, tile_act(act_ref, tile), NN, preferred_element_type=F32)
        gb_ref[n] = lax.dot_general(down, tile_og(og_ref, tile), NT, preferred_element_type=F32)
    for n, (b, a) in enumerate(places):
        e = domains[NEAR * a + b]
        o = e // 2
        i = e % 2
        ga = ga_ref[n]
        gb = gb_ref[n]
        at = pl.ds(pl.multiple_of(i * 32, 32), 32)
        acc_ref[o, at, :] += jnp.concatenate([ga[:, 0:128], ga[:, 128:256]], axis=0)
        acc_ref[o, 64:72, :] += jnp.where(block == 2 * i, gb[0:8], 0.0) + jnp.where(block == 2 * i + 1, gb[8:16], 0.0)


def first_kernel(ids_ref, act_ref, og_ref, in_ref, acc_ref, ga_ref, gb_ref):
    acc_ref[...] = jnp.zeros_like(acc_ref)
    add_grads(True, ids_ref, act_ref, og_ref, in_ref, acc_ref, ga_ref, gb_ref)


def second_kernel(ids_ref, act_ref, og_ref, in_ref, sum_ref, out_ref, acc_ref, ga_ref, gb_ref):
    acc_ref[...] = sum_ref[...]
    add_grads(False, ids_ref, act_ref, og_ref, in_ref, acc_ref, ga_ref, gb_ref)
    for o in range(OWNERS):
        out_ref[o] = (2.0 * acc_ref[o]).astype(BF16)


def final_kernel(in_ref, ga_ref, gb_ref):
    total = in_ref[0].astype(F32)
    for o in range(1, OWNERS):
        total = total + in_ref[o].astype(F32)
    for i in range(2):
        for h in range(2):
            ga_ref[i, :, 128 * h : 128 * h + 128] = total[32 * i + 16 * h : 32 * i + 16 * h + 16]
            k = 2 * i + h
            gb_ref[i, 8 * h : 8 * h + 8, :] = total[64:72, 32 * k : 32 * k + 32]


def shards(activations, out_grads, tile_domain, adapter_a, adapter_b):
    shape = jax.ShapeDtypeStruct
    ids = tile_domain.reshape(1, tile_domain.shape[0])
    og = out_grads.T
    pair = [(f, f ^ 1) for f in range(2 * SHARE)]
    near_groups = [[2 * (NEAR * a + b) + c for b in range(NEAR)] for a in range(FAR) for c in range(2)]
    far_groups = [[2 * (NEAR * a + b) + c for a in range(FAR)] for b in range(NEAR) for c in range(2)]
    near = lambda x: lax.all_to_all(x, "fsdp", 0, 0, tiled=True, axis_index_groups=near_groups)
    far = lambda x: lax.all_to_all(x, "fsdp", 0, 0, tiled=True, axis_index_groups=far_groups)
    swap = lambda x: lax.ppermute(x, "fsdp", pair)

    packed = call(
        pack_kernel,
        shape((OWNERS, ROWS, 128), BF16),
        [VMEM],
        jnp.concatenate([adapter_a, adapter_b], axis=2),
        cost=AHEAD,
    )
    weights = lax.all_to_all(packed, "dp", 0, 0, tiled=True)
    inputs = (ids, weights, activations, og)
    part = shape((NEAR, FAR * 32, 128), F32)
    kinds = [VMEM, VMEM, VMEM, VMEM]
    send = call(functools.partial(partial_kernel, False), part, kinds, *inputs, cost=HALF)
    keep = call(functools.partial(partial_kernel, True), part, kinds, *inputs, cost=HALF)
    scaled = shape((NEAR, SENT, 128), F32)
    chip = call(chip_kernel, scaled, [VMEM, VMEM], keep, swap(send), scratch=[pltpu.VMEM(part.shape, F32)])
    chip = near(chip.astype(F16)).astype(F32)
    part = call(near_kernel, shape((FAR, SENT, 128), F32), [VMEM], chip)
    part = far(part.astype(F16)).astype(F32)
    full = near(call(round_kernel, shape((NEAR, FAR * 32, 128), BF16), [VMEM], part))
    terms = [pltpu.VMEM((SHARE, 16, 256), F32), pltpu.VMEM((SHARE, 16, 128), F32)]
    total = (OWNERS, ROWS, 128)
    inputs = (ids, activations, og)
    grads = call(first_kernel, shape(total, F32), kinds, *inputs, full, scratch=terms, cost=HALF)
    grads = call(
        second_kernel, shape(total, BF16), kinds + [VMEM], *inputs, swap(full), grads, scratch=[pltpu.VMEM(total, F32)] + terms
    )
    summed = lax.all_to_all(grads, "dp", 0, 0, tiled=True)
    return call(final_kernel, (shape((2, RANK, 256), F32), shape((2, RANK, 32), F32)), [VMEM], summed)


def solution(mesh):
    placed = (
        P("dp", "fsdp"),
        P("dp", "fsdp"),
        P("dp", None),
        P("dp", None, "fsdp"),
        P("dp", None, "fsdp"),
    )
    return jax.shard_map(
        shards,
        mesh=mesh,
        in_specs=placed,
        out_specs=(P("dp", None, "fsdp"), P("dp", None, "fsdp")),
        check_vma=False,
    )
```

```python
import functools

import jax
import jax.numpy as jnp
from jax import lax
from jax.experimental import pallas as pl
from jax.experimental.pallas import tpu as pltpu
from jax.sharding import PartitionSpec as P

F32 = jnp.float32
BF16 = jnp.bfloat16
F16 = jnp.float16
TILE = 128
RANK = 16
OWNERS = 32
NEAR = 4
FAR = 4
SHARE = NEAR * FAR
ROWS = 72
SENT = FAR * 32 + 8
TOP = 16384.0

NT = (((1,), (1,)), ((), ()))
NN = (((1,), (0,)), ((), ()))
VMEM = pl.BlockSpec(memory_space=pltpu.VMEM)
MIB = 1024 * 1024
AHEAD = pl.CostEstimate(flops=10_000_000_000, bytes_accessed=20_000_000, transcendentals=0)
HALF = pl.CostEstimate(flops=2_000_000_000, bytes_accessed=4_000_000, transcendentals=0)


def call(kernel, out, specs, *operands, scratch=(), cost=None):
    return pl.pallas_call(
        kernel,
        out_shape=out,
        in_specs=specs,
        out_specs=jax.tree.map(lambda _: VMEM, out),
        scratch_shapes=scratch,
        cost_estimate=cost,
        compiler_params=pltpu.CompilerParams(vmem_limit_bytes=32 * MIB),
    )(*operands)


def lane_block():
    return lax.broadcasted_iota(jnp.int32, (8, 128), 1) // 32


def pack_kernel(ab_ref, out_ref):
    pieces = []
    for i in range(2):
        pieces += [ab_ref[i, :, 0:128], ab_ref[i, :, 128:256]]
    rows = lax.broadcasted_iota(jnp.int32, (32, 128), 0)
    lanes = lax.broadcasted_iota(jnp.int32, (32, 128), 1)
    small = jnp.zeros((8, 128), F32)
    for i in range(2):
        for h in range(2):
            place = jnp.where(lanes == rows + 32 * (2 * i + h), 1.0, 0.0).astype(BF16)
            spread = lax.dot_general(ab_ref[i, :, 256:288], place, NN, preferred_element_type=F32)
            small = small + spread[8 * h : 8 * h + 8]
    big = jnp.concatenate(pieces, axis=0)
    small = small.astype(BF16)
    for o in range(OWNERS):
        out_ref[o, 0:64] = big
        out_ref[o, 64:72] = small


def tile_at(b, a, parity):
    return 2 * NEAR * a + 2 * b + parity


def domains_of(ids_ref, parity):
    ids = ids_ref[...]
    return [jnp.where(parity == 1, ids[0, 2 * n + 1], ids[0, 2 * n]) for n in range(SHARE)]


def tile_og(og_ref, tile):
    og = og_ref[:, pl.ds(pl.multiple_of(tile * TILE, TILE), TILE)]
    return jnp.concatenate([og, og, og, og], axis=0)


def tile_act(act_ref, tile):
    return act_ref[pl.ds(pl.multiple_of(tile * TILE, TILE), TILE), :]


def scale_of(down_top, up_top):
    down = jnp.broadcast_to(jnp.max(down_top, axis=(0, 1), keepdims=True), (8, 128))
    up = jnp.broadcast_to(jnp.max(up_top, axis=(0, 1), keepdims=True), (8, 128))
    both = jnp.where(lax.broadcasted_iota(jnp.int32, (8, 128), 0) == 0, down, up)
    root = jnp.sqrt(jnp.sqrt(both))
    return jnp.maximum(root, 2.0**-13).astype(BF16).astype(F32)


def fourth(root):
    square = root * root
    return square * square


def widen(row):
    return jnp.broadcast_to(row, (16, 128))


def parity_of(own):
    core = lax.axis_index("fsdp") % 2
    return core if own else 1 - core


def partial_kernel(own, ids_ref, w_ref, act_ref, og_ref, out_ref):
    parity = parity_of(own)
    domains = domains_of(ids_ref, parity)
    block = lane_block()
    for b in range(NEAR):
        for a in range(FAR):
            tile = tile_at(b, a, parity)
            e = domains[NEAR * a + b]
            o = e // 2
            i = e % 2
            w = w_ref[o, pl.ds(pl.multiple_of(i * 32, 32), 32), :]
            small = w_ref[o, 64:72, :].astype(F32)
            left = jnp.concatenate([w[0:16], w[16:32]], axis=1)
            down = lax.dot_general(left, tile_act(act_ref, tile), NT, preferred_element_type=F32)
            spread = jnp.concatenate(
                [jnp.where(block == 2 * i, small, 0.0), jnp.where(block == 2 * i + 1, small, 0.0)], axis=0
            ).astype(BF16)
            up = lax.dot_general(spread, tile_og(og_ref, tile), NN, preferred_element_type=F32)
            out_ref[b, 32 * a : 32 * a + 16] = down
            out_ref[b, 32 * a + 16 : 32 * a + 32] = up


def chip_kernel(keep_ref, other_ref, out_ref, part_ref):
    down_top = jnp.zeros((RANK, TILE), F32)
    up_top = jnp.zeros((RANK, TILE), F32)
    for b in range(NEAR):
        part = keep_ref[b] + other_ref[b]
        part_ref[b] = part
        for a in range(FAR):
            down_top = jnp.maximum(down_top, jnp.abs(part[32 * a : 32 * a + 16]))
            up_top = jnp.maximum(up_top, jnp.abs(part[32 * a + 16 : 32 * a + 32]))
    root = scale_of(down_top, up_top)
    factor = TOP / fourth(root)
    both = jnp.concatenate([widen(factor[0:1]), widen(factor[1:2])] * FAR, axis=0)
    for b in range(NEAR):
        out_ref[b, 0 : FAR * 32] = part_ref[b] * both
        out_ref[b, FAR * 32 : SENT] = root


def summed_parts(in_ref, count):
    downs = [jnp.zeros((RANK, TILE), F32)] * FAR
    ups = [jnp.zeros((RANK, TILE), F32)] * FAR
    for q in range(count):
        factor = fourth(in_ref[q, FAR * 32 : SENT]) * (1.0 / TOP)
        down_factor, up_factor = widen(factor[0:1]), widen(factor[1:2])
        for a in range(FAR):
            downs[a] = downs[a] + in_ref[q, 32 * a : 32 * a + 16] * down_factor
            ups[a] = ups[a] + in_ref[q, 32 * a + 16 : 32 * a + 32] * up_factor
    return downs, ups


def near_kernel(in_ref, out_ref):
    sizes = [fourth(in_ref[q, FAR * 32 : SENT]) for q in range(NEAR)]
    root = jnp.sqrt(jnp.sqrt(sum(sizes[1:], sizes[0]))).astype(BF16).astype(F32)
    share = 1.0 / fourth(root)
    factors = []
    for size in sizes:
        factor = size * share
        factors.append((widen(factor[0:1]), widen(factor[1:2])))
    for a in range(FAR):
        at, to = 32 * a, 32 * a + 16
        down = in_ref[0, at:to] * factors[0][0]
        up = in_ref[0, to : to + 16] * factors[0][1]
        for q in range(1, NEAR):
            down = down + in_ref[q, at:to] * factors[q][0]
            up = up + in_ref[q, to : to + 16] * factors[q][1]
        for f in range(FAR):
            out_ref[f, at:to] = down
            out_ref[f, to : to + 16] = up
    for f in range(FAR):
        out_ref[f, FAR * 32 : SENT] = root


def round_kernel(in_ref, out_ref):
    downs, ups = summed_parts(in_ref, FAR)
    for a in range(FAR):
        down = downs[a].astype(BF16)
        up = ups[a].astype(BF16)
        for q in range(NEAR):
            out_ref[q, 32 * a : 32 * a + 16] = down
            out_ref[q, 32 * a + 16 : 32 * a + 32] = up


def add_grads(own, ids_ref, act_ref, og_ref, in_ref, acc_ref, ga_ref, gb_ref):
    parity = parity_of(own)
    domains = domains_of(ids_ref, parity)
    block = lane_block()
    places = [(b, a) for b in range(NEAR) for a in range(FAR)]
    for n, (b, a) in enumerate(places):
        tile = tile_at(b, a, parity)
        down = in_ref[b, 32 * a : 32 * a + 16]
        up = in_ref[b, 32 * a + 16 : 32 * a + 32]
        ga_ref[n] = lax.dot_general(up, tile_act(act_ref, tile), NN, preferred_element_type=F32)
        gb_ref[n] = lax.dot_general(down, tile_og(og_ref, tile), NT, preferred_element_type=F32)
    for n, (b, a) in enumerate(places):
        e = domains[NEAR * a + b]
        o = e // 2
        i = e % 2
        ga = ga_ref[n]
        gb = gb_ref[n]
        at = pl.ds(pl.multiple_of(i * 32, 32), 32)
        acc_ref[o, at, :] += jnp.concatenate([ga[:, 0:128], ga[:, 128:256]], axis=0)
        acc_ref[o, 64:72, :] += jnp.where(block == 2 * i, gb[0:8], 0.0) + jnp.where(block == 2 * i + 1, gb[8:16], 0.0)


def first_kernel(ids_ref, act_ref, og_ref, in_ref, acc_ref, ga_ref, gb_ref):
    acc_ref[...] = jnp.zeros_like(acc_ref)
    add_grads(True, ids_ref, act_ref, og_ref, in_ref, acc_ref, ga_ref, gb_ref)


def second_kernel(ids_ref, act_ref, og_ref, in_ref, sum_ref, out_ref, acc_ref, ga_ref, gb_ref):
    acc_ref[...] = sum_ref[...]
    add_grads(False, ids_ref, act_ref, og_ref, in_ref, acc_ref, ga_ref, gb_ref)
    for o in range(OWNERS):
        out_ref[o] = (2.0 * acc_ref[o]).astype(BF16)


def final_kernel(in_ref, ga_ref, gb_ref):
    total = in_ref[0].astype(F32)
    for o in range(1, OWNERS):
        total = total + in_ref[o].astype(F32)
    for i in range(2):
        for h in range(2):
            ga_ref[i, :, 128 * h : 128 * h + 128] = total[32 * i + 16 * h : 32 * i + 16 * h + 16]
            k = 2 * i + h
            gb_ref[i, 8 * h : 8 * h + 8, :] = total[64:72, 32 * k : 32 * k + 32]


def shards(activations, out_grads, tile_domain, adapter_a, adapter_b):
    shape = jax.ShapeDtypeStruct
    ids = tile_domain.reshape(1, tile_domain.shape[0])
    og = out_grads.T
    pair = [(f, f ^ 1) for f in range(2 * SHARE)]
    near_groups = [[2 * (NEAR * a + b) + c for b in range(NEAR)] for a in range(FAR) for c in range(2)]
    far_groups = [[2 * (NEAR * a + b) + c for a in range(FAR)] for b in range(NEAR) for c in range(2)]
    near = lambda x: lax.all_to_all(x, "fsdp", 0, 0, tiled=True, axis_index_groups=near_groups)
    far = lambda x: lax.all_to_all(x, "fsdp", 0, 0, tiled=True, axis_index_groups=far_groups)
    swap = lambda x: lax.ppermute(x, "fsdp", pair)

    packed = call(
        pack_kernel,
        shape((OWNERS, ROWS, 128), BF16),
        [VMEM],
        jnp.concatenate([adapter_a, adapter_b], axis=2),
        cost=AHEAD,
    )
    weights = lax.all_to_all(packed, "dp", 0, 0, tiled=True)
    inputs = (ids, weights, activations, og)
    part = shape((NEAR, FAR * 32, 128), F32)
    kinds = [VMEM, VMEM, VMEM, VMEM]
    send = call(functools.partial(partial_kernel, False), part, kinds, *inputs, cost=HALF)
    keep = call(functools.partial(partial_kernel, True), part, kinds, *inputs, cost=HALF)
    scaled = shape((NEAR, SENT, 128), F32)
    chip = call(chip_kernel, scaled, [VMEM, VMEM], keep, swap(send), scratch=[pltpu.VMEM(part.shape, F32)])
    chip = near(chip.astype(F16)).astype(F32)
    part = call(near_kernel, shape((FAR, SENT, 128), F32), [VMEM], chip)
    part = far(part.astype(F16)).astype(F32)
    full = near(call(round_kernel, shape((NEAR, FAR * 32, 128), BF16), [VMEM], part))
    terms = [pltpu.VMEM((SHARE, 16, 256), F32), pltpu.VMEM((SHARE, 16, 128), F32)]
    total = (OWNERS, ROWS, 128)
    inputs = (ids, activations, og)
    grads = call(first_kernel, shape(total, F32), kinds, *inputs, full, scratch=terms, cost=HALF)
    grads = call(
        second_kernel, shape(total, BF16), kinds + [VMEM], *inputs, swap(full), grads, scratch=[pltpu.VMEM(total, F32)] + terms
    )
    summed = lax.all_to_all(grads, "dp", 0, 0, tiled=True)
    return call(final_kernel, (shape((2, RANK, 256), F32), shape((2, RANK, 32), F32)), [VMEM], summed)


def solution(mesh):
    placed = (
        P("dp", "fsdp"),
        P("dp", "fsdp"),
        P("dp", None),
        P("dp", None, "fsdp"),
        P("dp", None, "fsdp"),
    )
    return jax.shard_map(
        shards,
        mesh=mesh,
        in_specs=placed,
        out_specs=(P("dp", None, "fsdp"), P("dp", None, "fsdp")),
        check_vma=False,
    )
```

```python
import functools

import jax
import jax.numpy as jnp
from jax import lax
from jax.experimental import pallas as pl
from jax.experimental.pallas import tpu as pltpu
from jax.sharding import PartitionSpec as P

F32 = jnp.float32
BF16 = jnp.bfloat16
F16 = jnp.float16
TILE = 128
RANK = 16
OWNERS = 32
NEAR = 4
FAR = 4
SHARE = NEAR * FAR
ROWS = 72
SENT = FAR * 32 + 8
TOP = 16384.0

NT = (((1,), (1,)), ((), ()))
NN = (((1,), (0,)), ((), ()))
VMEM = pl.BlockSpec(memory_space=pltpu.VMEM)
MIB = 1024 * 1024
AHEAD = pl.CostEstimate(flops=10_000_000_000, bytes_accessed=20_000_000, transcendentals=0)
HALF = pl.CostEstimate(flops=2_000_000_000, bytes_accessed=4_000_000, transcendentals=0)


def call(kernel, out, specs, *operands, scratch=(), cost=None):
    return pl.pallas_call(
        kernel,
        out_shape=out,
        in_specs=specs,
        out_specs=jax.tree.map(lambda _: VMEM, out),
        scratch_shapes=scratch,
        cost_estimate=cost,
        compiler_params=pltpu.CompilerParams(vmem_limit_bytes=32 * MIB),
    )(*operands)


def lane_block():
    return lax.broadcasted_iota(jnp.int32, (8, 128), 1) // 32


def pack_kernel(ab_ref, out_ref):
    pieces = []
    for i in range(2):
        pieces += [ab_ref[i, :, 0:128], ab_ref[i, :, 128:256]]
    rows = lax.broadcasted_iota(jnp.int32, (32, 128), 0)
    lanes = lax.broadcasted_iota(jnp.int32, (32, 128), 1)
    small = jnp.zeros((8, 128), F32)
    for i in range(2):
        for h in range(2):
            place = jnp.where(lanes == rows + 32 * (2 * i + h), 1.0, 0.0).astype(BF16)
            spread = lax.dot_general(ab_ref[i, :, 256:288], place, NN, preferred_element_type=F32)
            small = small + spread[8 * h : 8 * h + 8]
    big = jnp.concatenate(pieces, axis=0)
    small = small.astype(BF16)
    for o in range(OWNERS):
        out_ref[o, 0:64] = big
        out_ref[o, 64:72] = small


def tile_at(b, a, parity):
    return 2 * NEAR * a + 2 * b + parity


def domains_of(ids_ref, parity):
    ids = ids_ref[...]
    return [jnp.where(parity == 1, ids[0, 2 * n + 1], ids[0, 2 * n]) for n in range(SHARE)]


def tile_og(og_ref, tile):
    og = og_ref[:, pl.ds(pl.multiple_of(tile * TILE, TILE), TILE)]
    return jnp.concatenate([og, og, og, og], axis=0)


def tile_act(act_ref, tile):
    return act_ref[pl.ds(pl.multiple_of(tile * TILE, TILE), TILE), :]


def scale_of(down_top, up_top):
    down = jnp.broadcast_to(jnp.max(down_top, axis=(0, 1), keepdims=True), (8, 128))
    up = jnp.broadcast_to(jnp.max(up_top, axis=(0, 1), keepdims=True), (8, 128))
    both = jnp.where(lax.broadcasted_iota(jnp.int32, (8, 128), 0) == 0, down, up)
    root = jnp.sqrt(jnp.sqrt(both))
    return jnp.maximum(root, 2.0**-13).astype(BF16).astype(F32)


def fourth(root):
    square = root * root
    return square * square


def widen(row):
    return jnp.broadcast_to(row, (16, 128))


def parity_of(own):
    core = lax.axis_index("fsdp") % 2
    return core if own else 1 - core


def partial_kernel(own, ids_ref, w_ref, act_ref, og_ref, out_ref):
    parity = parity_of(own)
    domains = domains_of(ids_ref, parity)
    block = lane_block()
    for b in range(NEAR):
        for a in range(FAR):
            tile = tile_at(b, a, parity)
            e = domains[NEAR * a + b]
            o = e // 2
            i = e % 2
            w = w_ref[o, pl.ds(pl.multiple_of(i * 32, 32), 32), :]
            small = w_ref[o, 64:72, :].astype(F32)
            left = jnp.concatenate([w[0:16], w[16:32]], axis=1)
            down = lax.dot_general(left, tile_act(act_ref, tile), NT, preferred_element_type=F32)
            spread = jnp.concatenate(
                [jnp.where(block == 2 * i, small, 0.0), jnp.where(block == 2 * i + 1, small, 0.0)], axis=0
            ).astype(BF16)
            up = lax.dot_general(spread, tile_og(og_ref, tile), NN, preferred_element_type=F32)
            out_ref[b, 32 * a : 32 * a + 16] = down
            out_ref[b, 32 * a + 16 : 32 * a + 32] = up


def chip_kernel(keep_ref, other_ref, out_ref):
    down_top = jnp.zeros((RANK, TILE), F32)
    up_top = jnp.zeros((RANK, TILE), F32)
    for b in range(NEAR):
        part = keep_ref[b] + other_ref[b]
        for a in range(FAR):
            down_top = jnp.maximum(down_top, jnp.abs(part[32 * a : 32 * a + 16]))
            up_top = jnp.maximum(up_top, jnp.abs(part[32 * a + 16 : 32 * a + 32]))
    root = scale_of(down_top, up_top)
    factor = TOP / fourth(root)
    both = jnp.concatenate([widen(factor[0:1]), widen(factor[1:2])] * FAR, axis=0)
    for b in range(NEAR):
        out_ref[b, 0 : FAR * 32] = (keep_ref[b] + other_ref[b]) * both
        out_ref[b, FAR * 32 : SENT] = root


def summed_parts(in_ref, count):
    downs = [jnp.zeros((RANK, TILE), F32)] * FAR
    ups = [jnp.zeros((RANK, TILE), F32)] * FAR
    for q in range(count):
        factor = fourth(in_ref[q, FAR * 32 : SENT]) * (1.0 / TOP)
        down_factor, up_factor = widen(factor[0:1]), widen(factor[1:2])
        for a in range(FAR):
            downs[a] = downs[a] + in_ref[q, 32 * a : 32 * a + 16] * down_factor
            ups[a] = ups[a] + in_ref[q, 32 * a + 16 : 32 * a + 32] * up_factor
    return downs, ups


def near_kernel(in_ref, out_ref):
    downs, ups = summed_parts(in_ref, NEAR)
    down_top, up_top = jnp.abs(downs[0]), jnp.abs(ups[0])
    for a in range(1, FAR):
        down_top = jnp.maximum(down_top, jnp.abs(downs[a]))
        up_top = jnp.maximum(up_top, jnp.abs(ups[a]))
    root = scale_of(down_top, up_top)
    factor = TOP / fourth(root)
    down_factor, up_factor = widen(factor[0:1]), widen(factor[1:2])
    for a in range(FAR):
        down = downs[a] * down_factor
        up = ups[a] * up_factor
        for f in range(FAR):
            out_ref[f, 32 * a : 32 * a + 16] = down
            out_ref[f, 32 * a + 16 : 32 * a + 32] = up
    for f in range(FAR):
        out_ref[f, FAR * 32 : SENT] = root


def round_kernel(in_ref, out_ref):
    downs, ups = summed_parts(in_ref, FAR)
    for a in range(FAR):
        down = downs[a].astype(BF16)
        up = ups[a].astype(BF16)
        for q in range(NEAR):
            out_ref[q, 32 * a : 32 * a + 16] = down
            out_ref[q, 32 * a + 16 : 32 * a + 32] = up


def add_grads(own, ids_ref, act_ref, og_ref, in_ref, acc_ref, ga_ref, gb_ref):
    parity = parity_of(own)
    domains = domains_of(ids_ref, parity)
    block = lane_block()
    places = [(b, a) for b in range(NEAR) for a in range(FAR)]
    for n, (b, a) in enumerate(places):
        tile = tile_at(b, a, parity)
        down = in_ref[b, 32 * a : 32 * a + 16]
        up = in_ref[b, 32 * a + 16 : 32 * a + 32]
        ga_ref[n] = lax.dot_general(up, tile_act(act_ref, tile), NN, preferred_element_type=F32)
        gb_ref[n] = lax.dot_general(down, tile_og(og_ref, tile), NT, preferred_element_type=F32)
    for n, (b, a) in enumerate(places):
        e = domains[NEAR * a + b]
        o = e // 2
        i = e % 2
        ga = ga_ref[n]
        gb = gb_ref[n]
        at = pl.ds(pl.multiple_of(i * 32, 32), 32)
        acc_ref[o, at, :] += jnp.concatenate([ga[:, 0:128], ga[:, 128:256]], axis=0)
        acc_ref[o, 64:72, :] += jnp.where(block == 2 * i, gb[0:8], 0.0) + jnp.where(block == 2 * i + 1, gb[8:16], 0.0)


def first_kernel(ids_ref, act_ref, og_ref, in_ref, acc_ref, ga_ref, gb_ref):
    acc_ref[...] = jnp.zeros_like(acc_ref)
    add_grads(True, ids_ref, act_ref, og_ref, in_ref, acc_ref, ga_ref, gb_ref)


def second_kernel(ids_ref, act_ref, og_ref, in_ref, sum_ref, out_ref, acc_ref, ga_ref, gb_ref):
    acc_ref[...] = sum_ref[...]
    add_grads(False, ids_ref, act_ref, og_ref, in_ref, acc_ref, ga_ref, gb_ref)
    for o in range(OWNERS):
        out_ref[o] = (2.0 * acc_ref[o]).astype(BF16)


def final_kernel(in_ref, ga_ref, gb_ref):
    total = in_ref[0].astype(F32)
    for o in range(1, OWNERS):
        total = total + in_ref[o].astype(F32)
    for i in range(2):
        for h in range(2):
            ga_ref[i, :, 128 * h : 128 * h + 128] = total[32 * i + 16 * h : 32 * i + 16 * h + 16]
            k = 2 * i + h
            gb_ref[i, 8 * h : 8 * h + 8, :] = total[64:72, 32 * k : 32 * k + 32]


def shards(activations, out_grads, tile_domain, adapter_a, adapter_b):
    shape = jax.ShapeDtypeStruct
    ids = tile_domain.reshape(1, tile_domain.shape[0])
    og = out_grads.T
    pair = [(f, f ^ 1) for f in range(2 * SHARE)]
    near_groups = [[2 * (NEAR * a + b) + c for b in range(NEAR)] for a in range(FAR) for c in range(2)]
    far_groups = [[2 * (NEAR * a + b) + c for a in range(FAR)] for b in range(NEAR) for c in range(2)]
    near = lambda x: lax.all_to_all(x, "fsdp", 0, 0, tiled=True, axis_index_groups=near_groups)
    far = lambda x: lax.all_to_all(x, "fsdp", 0, 0, tiled=True, axis_index_groups=far_groups)
    swap = lambda x: lax.ppermute(x, "fsdp", pair)

    packed = call(
        pack_kernel,
        shape((OWNERS, ROWS, 128), BF16),
        [VMEM],
        jnp.concatenate([adapter_a, adapter_b], axis=2),
        cost=AHEAD,
    )
    weights = lax.all_to_all(packed, "dp", 0, 0, tiled=True)
    inputs = (ids, weights, activations, og)
    part = shape((NEAR, FAR * 32, 128), F32)
    kinds = [VMEM, VMEM, VMEM, VMEM]
    send = call(functools.partial(partial_kernel, False), part, kinds, *inputs, cost=HALF)
    keep = call(functools.partial(partial_kernel, True), part, kinds, *inputs, cost=HALF)
    scaled = shape((NEAR, SENT, 128), F32)
    chip = call(chip_kernel, scaled, [VMEM, VMEM], keep, swap(send))
    chip = near(chip.astype(F16)).astype(F32)
    part = call(near_kernel, shape((FAR, SENT, 128), F32), [VMEM], chip)
    part = far(part.astype(F16)).astype(F32)
    full = near(call(round_kernel, shape((NEAR, FAR * 32, 128), BF16), [VMEM], part))
    terms = [pltpu.VMEM((SHARE, 16, 256), F32), pltpu.VMEM((SHARE, 16, 128), F32)]
    total = (OWNERS, ROWS, 128)
    inputs = (ids, activations, og)
    grads = call(first_kernel, shape(total, F32), kinds, *inputs, full, scratch=terms, cost=HALF)
    grads = call(
        second_kernel, shape(total, BF16), kinds + [VMEM], *inputs, swap(full), grads, scratch=[pltpu.VMEM(total, F32)] + terms
    )
    summed = lax.all_to_all(grads, "dp", 0, 0, tiled=True)
    return call(final_kernel, (shape((2, RANK, 256), F32), shape((2, RANK, 32), F32)), [VMEM], summed)


def solution(mesh):
    placed = (
        P("dp", "fsdp"),
        P("dp", "fsdp"),
        P("dp", None),
        P("dp", None, "fsdp"),
        P("dp", None, "fsdp"),
    )
    return jax.shard_map(
        shards,
        mesh=mesh,
        in_specs=placed,
        out_specs=(P("dp", None, "fsdp"), P("dp", None, "fsdp")),
        check_vma=False,
    )
```
